32 devices in a mesh: groups: 2 (over x), inst: 4 (over z), dp: 4 (over y, core).
Axes of the slice: x: 2, y: 2, z: 4, core: 2. Of those that a mesh axis runs over, the one named last changes fastest.
Arguments:
- hidden: bfloat16 [16384, 7168], P(('groups', 'inst', 'dp')), parts along dimension 0, may hold values from -6 to 6
- input_gain: float32 [7168], replicated, may hold values from 0.1 to 1.9
- w_latent: bfloat16 [7168, 576], replicated, may hold values from -0.0625 to 0.0625
- latent_norm_gain: float32 [512], replicated, may hold values from 0.1 to 1.9
- req_len: int32 [8, 4, 4], P(('groups', 'inst'), 'dp'), parts along dimension 0, may hold values from 1 to 256, 512 in all within a row
- req_dest: int32 [8, 4, 4], P(('groups', 'inst'), 'dp'), parts along dimension 0, may hold values from 0 to 3, as said below
- req_block: int32 [8, 4, 4], P(('groups', 'inst'), 'dp'), parts along dimension 0, may hold values from 0 to 12, as said below
Outputs:
- decode_cache: bfloat16 [32768, 576], P(('groups', 'inst', 'dp')), parts along dimension 0
The draws below stay inside these ranges and needn't reach their ends.
There are 2 independent parts, one for each index of `groups`. The reference program is written for one: setup_inputs(seed, part) draws one part's arguments, and reference() takes and returns one part's arrays. A program takes and returns all parts, laid end to end along the dimension named above; an argument that names none is the same for every part. Nothing has to cross between parts.
Inputs may be any that keep to these rules, and one draw needn't show every extreme that they name: For each rank (i, d), req_dest[i, d, :] is a permutation of the 4 ranks. `req_block`: each is a multiple of 4; the requests that reach one decode device have different pages.
All inputs are finite; a program needn't handle non-finite values.
Results may differ from the reference program's by a relative error of at most 0.005.
Values may be sent and summed in bfloat16 or wider, within the bound.
A program may use at most 64 MiB of HBM per device.

```python
import math
import jax
import jax.numpy as jnp
import numpy as np
from jax import lax

D = 7168
LATENT_WIDTH = 512
BLOCK = 64
TOK_DEV = 512
LAT = 576
CAP = 256
CACHE_ROWS = 1024
TOKENS = 8192
N_INST = 4
N_DP = 4


def routing_tables(key):
    count = N_INST * N_DP
    keys = jax.random.split(key, count)
    dest = jax.vmap(lambda one: jax.random.permutation(one, N_DP))(keys).reshape(N_INST, N_DP, N_DP)
    other = jax.random.split(jax.random.fold_in(key, 7), count)
    order = jax.vmap(lambda one: jax.random.permutation(one, N_DP))(other).reshape(N_INST, N_DP, N_DP)
    flipped = jnp.transpose(order, (0, 2, 1))
    blocks = jnp.take_along_axis(flipped, dest, axis=2)
    return (dest.astype(jnp.int32), (blocks * ((CAP + BLOCK - 1) // BLOCK)).astype(jnp.int32))


def draw_req_dest(key, part):
    dest, blocks = routing_tables(key)
    return dest


def draw_req_block(key, part):
    dest, blocks = routing_tables(key)
    return blocks


def levels(own_key, extent, pieces, low, high):
    def one(position, shards_of):
        steps = jax.random.uniform(jax.random.fold_in(jax.random.fold_in(own_key, 6), position), (shards_of,), jnp.float32, low / len(pieces), high / len(pieces))
        return jnp.repeat(jnp.exp(steps), extent[position] // shards_of).reshape((-1,) + (1,) * (len(extent) - position - 1))

    level = one(*pieces[0])
    for cut in pieces[1:]:
        level = level * one(*cut)
    return level


def length_profile(number_of, total, bound, skew):
    weights = [(1 << 20) // math.isqrt(grade ** skew) + 1 for grade in range(2, number_of + 1)]
    rest, counts = total - bound - (number_of - 1), [1] * (number_of - 1)
    while rest > 0:
        free = [i for i in range(number_of - 1) if counts[i] < bound]
        whole, remaining = sum([weights[i] for i in free]), rest
        for i in free:
            extra = min(bound - counts[i], max(1, remaining * weights[i] // whole), rest)
            counts[i] = counts[i] + extra
            rest = rest - extra
    return np.array([bound] + counts)


def uneven_parts(own_key, count, total, most, slope):
    if count == 2:
        one = jax.random.randint(own_key, (), max(1, total - most), min(most, total - 1) + 1)
        return jnp.stack([one, total - one])
    sizes = jnp.asarray(length_profile(count, total, most, slope), jnp.int32)
    couples = (count - 1) // 2
    source_of, receiver = sizes[1:1 + 2 * couples:2], sizes[2:2 + 2 * couples:2]
    room = jnp.minimum(source_of - 1, most - receiver)
    shifted = jax.random.randint(jax.random.fold_in(own_key, 1), (couples,), 0, 1 << 20) % (room + 1)
    sizes = sizes.at[1:1 + 2 * couples:2].set(source_of - shifted).at[2:2 + 2 * couples:2].set(receiver + shifted)
    return sizes[jax.random.permutation(jax.random.fold_in(own_key, 2), count)]


def scatter_about(key, extent, width, limit, cuts=(), kind=jnp.bfloat16):
    level = levels(key, extent, cuts, -0.22, 0.18) if cuts else 1.0
    result = jax.random.normal(key, extent, jnp.float32) * width * level
    return jnp.minimum(jnp.maximum(result, -limit), limit).astype(kind)


def setup_inputs(seed: int = 0, part: int = 0) -> dict:
    streams_of = jax.random.split(jax.random.key(seed), 8)
    own_keys = jax.random.split(jax.random.fold_in(streams_of[7], part), 8)
    return {
        "hidden": scatter_about(own_keys[0], (TOKENS, D), 1.0, 6.0, ((0, 16),)),
        "input_gain": jnp.clip(1.0 + 0.18 * jax.random.normal(streams_of[1], (D,), jnp.float32), 0.1, 1.9),
        "w_latent": scatter_about(streams_of[2], (D, LAT), D ** -0.5, 0.0625),
        "latent_norm_gain": jnp.clip(1.0 + 0.18 * jax.random.normal(streams_of[3], (LATENT_WIDTH,), jnp.float32), 0.1, 1.9),
        "req_len": jax.vmap(lambda own: uneven_parts(own, N_DP, TOK_DEV, CAP, 2))(jax.random.split(own_keys[4], N_INST * N_DP)).reshape((N_INST, N_DP, N_DP)).astype(jnp.int32),
        "req_dest": draw_req_dest(jax.random.fold_in(jax.random.fold_in(streams_of[7], part), 71), part),
        "req_block": draw_req_block(jax.random.fold_in(jax.random.fold_in(streams_of[7], part), 71), part),
    }


def apply_rotary(rot, pos):
    half = rot.shape[-1] // 2
    inv = 10000.0 ** (-jnp.arange(half, dtype=jnp.float32) / half)
    angle = pos[:, None] * inv[None, :]
    first = rot[:, :half]
    second = rot[:, half:]
    cosv = jnp.cos(angle)
    sinv = jnp.sin(angle)
    return jnp.concatenate([first * cosv - second * sinv, first * sinv + second * cosv], axis=1)

def reference(hidden, input_gain, w_latent, latent_norm_gain, req_len, req_dest, req_block):
    xf = hidden.astype(jnp.float32)
    scale = jax.lax.rsqrt(lax.optimization_barrier(jnp.mean(xf * xf, axis=1, keepdims=True)) + 1e-06)
    normed = (xf * scale * input_gain[None, :]).astype(jnp.bfloat16)
    latent_vectors = jnp.dot(normed, w_latent, preferred_element_type=jnp.float32)
    lens = req_len.reshape(N_INST * N_DP, N_DP)
    ends = jnp.cumsum(lens, axis=1)
    starts = ends - lens
    rowpos = jnp.arange(TOK_DEV, dtype=jnp.int32)
    inside = (rowpos[None, :, None] >= starts[:, None, :]) & (rowpos[None, :, None] < ends[:, None, :])
    inside = inside.astype(jnp.int32)
    start_tok = lax.optimization_barrier(jnp.sum(inside * starts[:, None, :], axis=2))
    dest_tok = lax.optimization_barrier(jnp.sum(inside * req_dest.reshape(N_INST * N_DP, N_DP)[:, None, :], axis=2))
    block_tok = lax.optimization_barrier(jnp.sum(inside * req_block.reshape(N_INST * N_DP, N_DP)[:, None, :], axis=2))
    pos = rowpos[None, :] - start_tok
    src = jnp.arange(N_INST * N_DP, dtype=jnp.int32)
    dest_inst = (src // N_DP + N_INST // 2) % N_INST
    device = dest_inst[:, None] * N_DP + dest_tok
    target = (device * CACHE_ROWS + block_tok * BLOCK + pos).reshape(-1)
    position_float = pos.reshape(-1).astype(jnp.float32)
    key_value_input = latent_vectors[:, :LATENT_WIDTH]
    key_value_input = key_value_input * jax.lax.rsqrt(lax.optimization_barrier(jnp.mean(key_value_input * key_value_input, axis=1, keepdims=True)) + 1e-06) * latent_norm_gain[None, :]
    cache_rows_out = jnp.concatenate([key_value_input, apply_rotary(latent_vectors[:, LATENT_WIDTH:], position_float)], axis=1).astype(jnp.bfloat16)
    cache = jnp.zeros((N_INST * N_DP * CACHE_ROWS, LAT), jnp.bfloat16)
    return cache.at[target.astype(jnp.int32)].set(cache_rows_out)
```

```python
import functools
import math

import jax
import jax.numpy as jnp
from jax import lax
from jax.experimental import pallas as pl
from jax.experimental.pallas import tpu as pltpu
from jax.sharding import PartitionSpec as P

BLOCK = 64
LANES = 128
MESH = pl.DeviceIdType.MESH
CHUNKS = (128, 128, 128, 128)
KTILE = 1024


def kernel(
    sizes,
    len_ref,
    dest_ref,
    block_ref,
    gain_ref,
    norm_ref,
    x_ref,
    w_ref,
    out_ref,
    x_v,
    w_v,
    acc,
    trig,
    mine,
    held,
    meta_mine,
    meta_held,
    meta_smem,
    x_sem,
    w_sem,
    z_sem,
    pass_sem,
    relay_sem,
    recv_sem,
    meta_send,
    meta_recv,
    meta_local,
):
    n_inst, n_dp = sizes
    tokens, width = x_v.shape
    latent = norm_ref.shape[1]
    rotary = w_ref.shape[1] - latent
    half = rotary // 2
    pieces = latent // LANES
    capacity = 2 * tokens // n_dp
    n_y = n_dp // 2
    steps = len(CHUNKS)
    first_row = [sum(CHUNKS[:c]) for c in range(steps)]

    def packed(rows):
        return rows * (latent + rotary) // LANES

    group = lax.axis_index("groups")
    inst = lax.axis_index("inst")
    rank = lax.axis_index("dp")
    far = lax.rem(inst + n_inst // 2, n_inst)
    y = rank // 2
    core = lax.rem(rank, 2)
    sibling = y * 2 + 1 - core
    columns = [lax.rem(y + j, n_y) * 2 + core for j in range(1, n_y)]

    w_copies = [
        pltpu.make_async_copy(
            w_ref.at[pl.ds(k * KTILE, KTILE), :], w_v.at[pl.ds(k * KTILE, KTILE), :], w_sem.at[k]
        )
        for k in range(width // KTILE)
    ]
    x_copies = [
        pltpu.make_async_copy(
            x_ref.at[pl.ds(first_row[c], CHUNKS[c]), :],
            x_v.at[pl.ds(first_row[c], CHUNKS[c]), :],
            x_sem.at[c],
        )
        for c in range(steps)
    ]
    x_copies[0].start()
    for copy in w_copies:
        copy.start()
    for copy in x_copies[1:]:
        copy.start()

    barrier = pltpu.get_barrier_semaphore()
    for e in range(n_dp):
        pl.semaphore_signal(barrier, inc=1, device_id=(group, far, e), device_id_type=MESH)
    for other in [sibling] + columns:
        pl.semaphore_signal(barrier, inc=1, device_id=(group, inst, other), device_id_type=MESH)

    starts = []
    total = jnp.int32(0)
    for k in range(n_dp):
        starts.append(total)
        total = total + len_ref[0, 0, k]
    row = lax.broadcasted_iota(jnp.int32, meta_mine.shape, 0)
    lane = lax.broadcasted_iota(jnp.int32, meta_mine.shape, 1)
    table = jnp.zeros(meta_mine.shape, jnp.int32)
    for k in range(n_dp):
        entry = jnp.where(
            lane == 0,
            starts[k],
            jnp.where(lane == 1, len_ref[0, 0, k], block_ref[0, 0, k]),
        )
        table = jnp.where(row == dest_ref[0, 0, k], entry, table)
    meta_mine[...] = table

    turn = lax.broadcasted_iota(jnp.int32, (tokens, LANES), 1)
    which = lax.rem(turn, half).astype(jnp.float32)
    inverse = jnp.exp(which * jnp.float32(-math.log(10000.0) / half))
    at = lax.broadcasted_iota(jnp.int32, (tokens, LANES), 0)
    begin = jnp.zeros((tokens, LANES), jnp.int32)
    for k in range(1, n_dp):
        begin = jnp.where(at >= starts[k], starts[k], begin)
    angle = (at - begin).astype(jnp.float32) * inverse
    angle = jnp.where(turn < rotary, angle, angle - jnp.float32(math.pi / 2))
    trig[...] = jnp.cos(angle)

    def compute(c):
        rows = CHUNKS[c]
        span = pl.ds(first_row[c], rows)
        x_copies[c].wait()
        acc[pl.ds(0, rows), :] = jnp.zeros((rows, acc.shape[1]), jnp.float32)
        squares = jnp.zeros((rows, 1), jnp.float32)
        for k in range(width // KTILE):
            if c == 0:
                w_copies[k].wait()
            cols = pl.ds(k * KTILE, KTILE)
            values = x_v[span, cols].astype(jnp.float32)
            squares = squares + jnp.sum(values * values, axis=1, keepdims=True)
            scaled = (values * gain_ref[:, cols]).astype(jnp.bfloat16)
            acc[pl.ds(0, rows), :] += jnp.dot(
                scaled, w_v[cols, :], preferred_element_type=jnp.float32
            )
        scale = lax.rsqrt(squares * (1.0 / width) + 1e-06)
        compressed = acc[pl.ds(0, rows), pl.ds(0, latent)] * scale
        power = jnp.mean(compressed * compressed, axis=1, keepdims=True)
        compressed = compressed * lax.rsqrt(power + 1e-06) * norm_ref[...]
        compressed = compressed.astype(jnp.bfloat16)
        base = packed(first_row[c])
        for j in range(pieces):
            mine[pl.ds(base + j * rows, rows), :] = compressed[:, j * LANES : (j + 1) * LANES]
        turned = acc[pl.ds(0, rows), pl.ds(latent, rotary)] * scale
        a, b = turned[:, :half], turned[:, half:]
        cosine = trig[span, pl.ds(0, half)]
        sine = trig[span, pl.ds(rotary, half)]
        turned = jnp.concatenate([a * cosine - b * sine, a * sine + b * cosine], axis=1)
        turned = jnp.concatenate([turned[: rows // 2], turned[rows // 2 :]], axis=1)
        mine[pl.ds(base + pieces * rows, rows // 2), :] = turned.astype(jnp.bfloat16)

    def chunk_of(c):
        return pl.ds(packed(first_row[c]), packed(CHUNKS[c]))

    def send_far(c):
        return pltpu.make_async_remote_copy(
            src_ref=mine.at[chunk_of(c)],
            dst_ref=held.at[rank, chunk_of(c)],
            send_sem=z_sem.at[c],
            recv_sem=recv_sem.at[rank, c],
            device_id=(group, far, rank),
            device_id_type=MESH,
        )

    def pass_on(c, source, target, sem):
        return pltpu.make_async_remote_copy(
            src_ref=held.at[source, chunk_of(c)],
            dst_ref=held.at[source, chunk_of(c)],
            send_sem=sem,
            recv_sem=recv_sem.at[source, c],
            device_id=(group, inst, target),
            device_id_type=MESH,
        )

    def send_meta(e, source):
        return pltpu.make_async_remote_copy(
            src_ref=meta_mine,
            dst_ref=meta_held.at[source],
            send_sem=meta_send.at[e],
            recv_sem=meta_recv.at[source],
            device_id=(group, far, e),
            device_id_type=MESH,
        )

    for c in range(steps):
        compute(c)
        if c == 0:
            pl.semaphore_wait(barrier, n_dp + 1 + len(columns))
        send_far(c).start()
        if c == 0:
            for e in range(n_dp):
                send_meta(e, rank).start()

    def spread(c):
        send_far(c).wait_recv()
        for j, other in enumerate(columns):
            pass_on(c, rank, other, pass_sem.at[j, c]).start()
        pass_on(c, rank, sibling, pass_sem.at[n_y - 1, c]).start()

    def relay(c):
        for j, other in enumerate(columns):
            pass_on(c, other, other, relay_sem.at[j, c]).wait_recv()
            pass_on(c, other, sibling, relay_sem.at[j, c]).start()

    for c in range(steps):
        spread(c)
        if c == 0:
            for d in range(n_dp):
                send_meta(0, d).wait_recv()
            to_smem = pltpu.make_async_copy(meta_held, meta_smem, meta_local)
            to_smem.start()
            to_smem.wait()
        if c > 0:
            relay(c - 1)
    relay(steps - 1)
    for c in range(steps):
        for source in [sibling] + [o // 2 * 2 + 1 - core for o in columns]:
            pass_on(c, source, sibling, pass_sem.at[0, c]).wait_recv()

    for b in range(n_dp):
        page = b * (capacity // BLOCK)
        source, start, count = jnp.int32(0), jnp.int32(0), jnp.int32(0)
        for d in range(n_dp):
            here = meta_smem[d, rank, 2] == page
            source = jnp.where(here, d, source)
            start = jnp.where(here, meta_smem[d, rank, 0], start)
            count = jnp.where(here, meta_smem[d, rank, 1], count)
        out_row = lax.broadcasted_iota(jnp.int32, (capacity, tokens), 0)
        in_row = lax.broadcasted_iota(jnp.int32, (capacity, tokens), 1)
        pick = (in_row == out_row + start) & (out_row < count)
        pick = jnp.where(pick, 1.0, 0.0).astype(jnp.bfloat16)
        left, right = [], []
        for c in range(steps):
            base, rows = packed(first_row[c]), CHUNKS[c]
            left.append(
                jnp.concatenate(
                    [held[source, pl.ds(base + j * rows, rows), :] for j in range(pieces)], axis=1
                )
            )
            both = held[source, pl.ds(base + pieces * rows, rows // 2), :]
            right.append(both[:, :rotary])
            right.append(both[:, rotary:])
        left = jnp.concatenate(left, axis=0)
        right = jnp.concatenate(right, axis=0)
        place = pl.ds(b * capacity, capacity)
        out_ref[place, pl.ds(0, latent)] = jnp.dot(
            pick, left, preferred_element_type=jnp.float32
        ).astype(out_ref.dtype)
        out_ref[place, pl.ds(latent, rotary)] = jnp.dot(
            pick, right, preferred_element_type=jnp.float32
        ).astype(out_ref.dtype)

    for e in range(n_dp):
        send_meta(e, rank).wait_send()
    for c in range(steps):
        send_far(c).wait_send()
        for j, other in enumerate(columns):
            pass_on(c, rank, other, pass_sem.at[j, c]).wait_send()
            pass_on(c, other, sibling, relay_sem.at[j, c]).wait_send()
        pass_on(c, rank, sibling, pass_sem.at[n_y - 1, c]).wait_send()


def on_device(
    n_inst, n_dp, hidden, input_gain, w_latent, latent_norm_gain, req_len, req_dest, req_block
):
    tokens, width = hidden.shape
    lat = w_latent.shape[1]
    latent = latent_norm_gain.shape[0]
    steps = len(CHUNKS)
    n_y = n_dp // 2
    words = tokens * lat // LANES
    meta_rows = max(8, n_dp)
    smem = pl.BlockSpec(memory_space=pltpu.SMEM)
    vmem = pl.BlockSpec(memory_space=pltpu.VMEM)
    hbm = pl.BlockSpec(memory_space=pl.ANY)
    dma = pltpu.SemaphoreType.DMA
    return pl.pallas_call(
        functools.partial(kernel, (n_inst, n_dp)),
        out_shape=jax.ShapeDtypeStruct((2 * tokens, lat), jnp.bfloat16),
        in_specs=[smem, smem, smem, vmem, vmem, hbm, hbm],
        out_specs=vmem,
        scratch_shapes=[
            pltpu.VMEM((tokens, width), jnp.bfloat16),
            pltpu.VMEM((width, lat), jnp.bfloat16),
            pltpu.VMEM((max(CHUNKS), lat), jnp.float32),
            pltpu.VMEM((tokens, LANES), jnp.float32),
            pltpu.VMEM((words, LANES), jnp.bfloat16),
            pltpu.VMEM((n_dp, words, LANES), jnp.bfloat16),
            pltpu.VMEM((meta_rows, LANES), jnp.int32),
            pltpu.VMEM((n_dp, meta_rows, LANES), jnp.int32),
            pltpu.SMEM((n_dp, meta_rows, LANES), jnp.int32),
            dma((steps,)),
            dma((width // KTILE,)),
            dma((steps,)),
            dma((n_y, steps)),
            dma((n_y, steps)),
            dma((n_dp, steps)),
            dma((n_dp,)),
            dma((n_dp,)),
            dma,
        ],
        compiler_params=pltpu.CompilerParams(
            collective_id=0, has_side_effects=True, vmem_limit_bytes=48 * 1024 * 1024
        ),
        cost_estimate=pl.CostEstimate(
            flops=2 * tokens * width * lat,
            bytes_accessed=2 * (tokens * width + width * lat + 2 * tokens * lat),
            transcendentals=tokens * LANES,
        ),
    )(
        req_len,
        req_dest,
        req_block,
        input_gain.reshape(1, width),
        latent_norm_gain.reshape(1, latent),
        hidden,
        w_latent,
    )


def solution(mesh):
    placed = (
        P(("groups", "inst", "dp"), None),
        P(),
        P(),
        P(),
        P(("groups", "inst"), "dp", None),
        P(("groups", "inst"), "dp", None),
        P(("groups", "inst"), "dp", None),
    )
    return jax.shard_map(
        functools.partial(on_device, mesh.shape["inst"], mesh.shape["dp"]),
        mesh=mesh,
        in_specs=placed,
        out_specs=P(("groups", "inst", "dp"), None),
        check_vma=False,
    )
```

```python
import functools
import math

import jax
import jax.numpy as jnp
from jax import lax
from jax.experimental import pallas as pl
from jax.experimental.pallas import tpu as pltpu
from jax.sharding import PartitionSpec as P

BLOCK = 64
LANES = 128
MESH = pl.DeviceIdType.MESH
CHUNKS = (128, 128, 256)
SPLIT = 2
KTILE = 1024


def kernel(
    sizes,
    len_ref,
    dest_ref,
    block_ref,
    gain_ref,
    norm_ref,
    x_ref,
    w_ref,
    out_ref,
    x_v,
    w_v,
    acc,
    trig,
    norm,
    mine,
    held,
    meta_mine,
    meta_held,
    meta_smem,
    x_sem,
    w_sem,
    z_sem,
    pass_sem,
    relay_sem,
    recv_sem,
    meta_send,
    meta_recv,
    meta_local,
):
    n_inst, n_dp = sizes
    units, tokens, width = mine.shape[0], x_v.shape[0], x_v.shape[1]
    features = w_ref.shape[0]
    latent = norm_ref.shape[1]
    half = (features - latent) // 2
    capacity = 2 * tokens // n_dp
    n_y = n_dp // 2
    steps = units * SPLIT
    part = features // SPLIT
    first_row = [sum(CHUNKS[:c]) for c in range(len(CHUNKS))]

    group = lax.axis_index("groups")
    inst = lax.axis_index("inst")
    rank = lax.axis_index("dp")
    far = lax.rem(inst + n_inst // 2, n_inst)
    y = rank // 2
    core = lax.rem(rank, 2)
    sibling = y * 2 + 1 - core
    columns = [lax.rem(y + j, n_y) * 2 + core for j in range(1, n_y)]

    w_copies = [
        pltpu.make_async_copy(
            w_ref.at[:, pl.ds(k * KTILE, KTILE)], w_v.at[:, pl.ds(k * KTILE, KTILE)], w_sem.at[k]
        )
        for k in range(width // KTILE)
    ]
    x_copies = [
        pltpu.make_async_copy(
            x_ref.at[pl.ds(first_row[c], CHUNKS[c]), :],
            x_v.at[pl.ds(first_row[c], CHUNKS[c]), :],
            x_sem.at[c],
        )
        for c in range(len(CHUNKS))
    ]
    x_copies[0].start()
    for copy in w_copies:
        copy.start()
    for copy in x_copies[1:]:
        copy.start()

    barrier = pltpu.get_barrier_semaphore()
    for e in range(n_dp):
        pl.semaphore_signal(barrier, inc=1, device_id=(group, far, e), device_id_type=MESH)
    for other in [sibling] + columns:
        pl.semaphore_signal(barrier, inc=1, device_id=(group, inst, other), device_id_type=MESH)

    starts = []
    total = jnp.int32(0)
    for k in range(n_dp):
        starts.append(total)
        total = total + len_ref[0, 0, k]
    row = lax.broadcasted_iota(jnp.int32, meta_mine.shape, 0)
    lane = lax.broadcasted_iota(jnp.int32, meta_mine.shape, 1)
    table = jnp.zeros(meta_mine.shape, jnp.int32)
    for k in range(n_dp):
        entry = jnp.where(
            lane == 0,
            starts[k],
            jnp.where(lane == 1, len_ref[0, 0, k], block_ref[0, 0, k]),
        )
        table = jnp.where(row == dest_ref[0, 0, k], entry, table)
    meta_mine[...] = table

    which = lax.broadcasted_iota(jnp.int32, (half, tokens), 0).astype(jnp.float32)
    inverse = jnp.exp(which * jnp.float32(-math.log(10000.0) / half))
    at = lax.broadcasted_iota(jnp.int32, (half, tokens), 1)
    begin = jnp.zeros((half, tokens), jnp.int32)
    for k in range(1, n_dp):
        begin = jnp.where(at >= starts[k], starts[k], begin)
    angle = (at - begin).astype(jnp.float32) * inverse
    trig[pl.ds(0, half), :] = jnp.cos(angle)
    trig[pl.ds(half, half), :] = jnp.sin(angle)

    norm[...] = jnp.broadcast_to(norm_ref[...], (LANES, latent)).T

    def compute(c):
        rows = CHUNKS[c]
        span = pl.ds(first_row[c], rows)
        x_copies[c].wait()
        squares = jnp.zeros((rows, LANES), jnp.float32)
        for k in range(width // KTILE):
            if c == 0:
                w_copies[k].wait()
            cols = pl.ds(k * KTILE, KTILE)
            values = x_v[span, cols].astype(jnp.float32)
            powers = values * values
            for j in range(KTILE // LANES):
                squares = squares + powers[:, j * LANES : (j + 1) * LANES]
            scaled = (values * gain_ref[:, cols]).astype(jnp.bfloat16)
            product = lax.dot_general(
                w_v[:, cols],
                scaled,
                (((1,), (1,)), ((), ())),
                preferred_element_type=jnp.float32,
            )
            if k == 0:
                acc[:, pl.ds(0, rows)] = product
            else:
                acc[:, pl.ds(0, rows)] += product
        squares = jnp.sum(squares.T, axis=0, keepdims=True)
        scale = lax.rsqrt(squares * (1.0 / width) + 1e-06)
        compressed = acc[pl.ds(0, latent), pl.ds(0, rows)] * scale
        power = jnp.mean(compressed * compressed, axis=0, keepdims=True)
        compressed = compressed * lax.rsqrt(power + 1e-06)
        a = acc[pl.ds(latent, half), pl.ds(0, rows)] * scale
        b = acc[pl.ds(latent + half, half), pl.ds(0, rows)] * scale
        cosine, sine = trig[pl.ds(0, half), span], trig[pl.ds(half, half), span]
        turned = jnp.concatenate([a * cosine - b * sine, a * sine + b * cosine], axis=0)
        for u in range(rows // LANES):
            lanes = slice(u * LANES, (u + 1) * LANES)
            unit = first_row[c] // LANES + u
            mine[unit, pl.ds(0, latent), :] = (compressed[:, lanes] * norm[...]).astype(jnp.bfloat16)
            mine[unit, pl.ds(latent, 2 * half), :] = turned[:, lanes].astype(jnp.bfloat16)

    def rows_of(s):
        return pl.ds((s % SPLIT) * part, part)

    def send_far(s):
        return pltpu.make_async_remote_copy(
            src_ref=mine.at[s // SPLIT, rows_of(s)],
            dst_ref=held.at[rank, s // SPLIT, rows_of(s)],
            send_sem=z_sem.at[s],
            recv_sem=recv_sem.at[rank, s],
            device_id=(group, far, rank),
            device_id_type=MESH,
        )

    def pass_on(c, source, target, sem):
        return pltpu.make_async_remote_copy(
            src_ref=held.at[source, c // SPLIT, rows_of(c)],
            dst_ref=held.at[source, c // SPLIT, rows_of(c)],
            send_sem=sem,
            recv_sem=recv_sem.at[source, c],
            device_id=(group, inst, target),
            device_id_type=MESH,
        )

    def send_meta(e, source):
        return pltpu.make_async_remote_copy(
            src_ref=meta_mine,
            dst_ref=meta_held.at[source],
            send_sem=meta_send.at[e],
            recv_sem=meta_recv.at[source],
            device_id=(group, far, e),
            device_id_type=MESH,
        )

    for c in range(len(CHUNKS)):
        compute(c)
        if c == 0:
            pl.semaphore_wait(barrier, n_dp + 1 + len(columns))
        for s in range(CHUNKS[c] // LANES * SPLIT):
            send_far(first_row[c] // LANES * SPLIT + s).start()
        if c == 0:
            for e in range(n_dp):
                send_meta(e, rank).start()

    def spread(c):
        send_far(c).wait_recv()
        for j, other in enumerate(columns):
            pass_on(c, rank, other, pass_sem.at[j, c]).start()
        pass_on(c, rank, sibling, pass_sem.at[n_y - 1, c]).start()

    def relay(c):
        for j, other in enumerate(columns):
            pass_on(c, other, other, relay_sem.at[j, c]).wait_recv()
            pass_on(c, other, sibling, relay_sem.at[j, c]).start()

    for c in range(steps):
        spread(c)
        if c == 0:
            for d in range(n_dp):
                send_meta(0, d).wait_recv()
            to_smem = pltpu.make_async_copy(meta_held, meta_smem, meta_local)
            to_smem.start()
            to_smem.wait()
        if c > 0:
            relay(c - 1)
    relay(steps - 1)
    for c in range(steps):
        for source in [sibling] + [o // 2 * 2 + 1 - core for o in columns]:
            pass_on(c, source, sibling, pass_sem.at[0, c]).wait_recv()

    together = max(1, LANES // capacity)
    for first in range(0, n_dp, together):
        blocks = []
        for b in range(first, first + together):
            page = b * (capacity // BLOCK)
            source, start, count = jnp.int32(0), jnp.int32(0), jnp.int32(0)
            for d in range(n_dp):
                here = meta_smem[d, rank, 2] == page
                source = jnp.where(here, d, source)
                start = jnp.where(here, meta_smem[d, rank, 0], start)
                count = jnp.where(here, meta_smem[d, rank, 1], count)
            in_row = lax.broadcasted_iota(jnp.int32, (tokens, capacity), 0)
            out_row = lax.broadcasted_iota(jnp.int32, (tokens, capacity), 1)
            pick = (in_row == out_row + start) & (out_row < count)
            pick = jnp.where(pick, 1.0, 0.0).astype(jnp.bfloat16)
            rows = jnp.concatenate([held[source, u] for u in range(units)], axis=1)
            blocks.append(jnp.dot(rows, pick, preferred_element_type=jnp.float32))
        block = blocks[0] if together == 1 else jnp.concatenate(blocks, axis=1)
        out_ref[:, pl.ds(first * capacity, together * capacity)] = block.astype(out_ref.dtype)

    for e in range(n_dp):
        send_meta(e, rank).wait_send()
    for c in range(steps):
        send_far(c).wait_send()
        for j, other in enumerate(columns):
            pass_on(c, rank, other, pass_sem.at[j, c]).wait_send()
            pass_on(c, other, sibling, relay_sem.at[j, c]).wait_send()
        pass_on(c, rank, sibling, pass_sem.at[n_y - 1, c]).wait_send()


def on_device(
    n_inst, n_dp, hidden, input_gain, w_latent, latent_norm_gain, req_len, req_dest, req_block
):
    tokens, width = hidden.shape
    lat = w_latent.shape[1]
    latent = latent_norm_gain.shape[0]
    units = tokens // LANES
    steps = units * SPLIT
    n_y = n_dp // 2
    meta_rows = max(8, n_dp)
    smem = pl.BlockSpec(memory_space=pltpu.SMEM)
    vmem = pl.BlockSpec(memory_space=pltpu.VMEM)
    hbm = pl.BlockSpec(memory_space=pl.ANY)
    dma = pltpu.SemaphoreType.DMA
    placed = pl.pallas_call(
        functools.partial(kernel, (n_inst, n_dp)),
        out_shape=jax.ShapeDtypeStruct((lat, 2 * tokens), jnp.bfloat16),
        in_specs=[smem, smem, smem, vmem, vmem, hbm, hbm],
        out_specs=vmem,
        scratch_shapes=[
            pltpu.VMEM((tokens, width), jnp.bfloat16),
            pltpu.VMEM((lat, width), jnp.bfloat16),
            pltpu.VMEM((lat, max(CHUNKS)), jnp.float32),
            pltpu.VMEM((lat - latent, tokens), jnp.float32),
            pltpu.VMEM((latent, LANES), jnp.float32),
            pltpu.VMEM((units, lat, LANES), jnp.bfloat16),
            pltpu.VMEM((n_dp, units, lat, LANES), jnp.bfloat16),
            pltpu.VMEM((meta_rows, LANES), jnp.int32),
            pltpu.VMEM((n_dp, meta_rows, LANES), jnp.int32),
            pltpu.SMEM((n_dp, meta_rows, LANES), jnp.int32),
            dma((len(CHUNKS),)),
            dma((width // KTILE,)),
            dma((steps,)),
            dma((n_y, steps)),
            dma((n_y, steps)),
            dma((n_dp, steps)),
            dma((n_dp,)),
            dma((n_dp,)),
            dma,
        ],
        compiler_params=pltpu.CompilerParams(
            collective_id=0, has_side_effects=True, vmem_limit_bytes=48 * 1024 * 1024
        ),
        cost_estimate=pl.CostEstimate(
            flops=2 * tokens * width * lat,
            bytes_accessed=2 * (tokens * width + width * lat + 2 * tokens * lat),
            transcendentals=tokens * LANES,
        ),
    )(
        req_len,
        req_dest,
        req_block,
        input_gain.reshape(1, width),
        latent_norm_gain.reshape(1, latent),
        hidden,
        w_latent.T,
    )
    return placed.T


def solution(mesh):
    placed = (
        P(("groups", "inst", "dp"), None),
        P(),
        P(),
        P(),
        P(("groups", "inst"), "dp", None),
        P(("groups", "inst"), "dp", None),
        P(("groups", "inst"), "dp", None),
    )
    return jax.shard_map(
        functools.partial(on_device, mesh.shape["inst"], mesh.shape["dp"]),
        mesh=mesh,
        in_specs=placed,
        out_specs=P(("groups", "inst", "dp"), None),
        check_vma=False,
    )
```

```python
import functools
import math

import jax
import jax.numpy as jnp
from jax import lax
from jax.experimental import pallas as pl
from jax.experimental.pallas import tpu as pltpu
from jax.sharding import PartitionSpec as P

BLOCK = 64
LANES = 128
MESH = pl.DeviceIdType.MESH
CHUNKS = (128, 128, 128, 128)
KTILE = 1024


def kernel(
    sizes,
    len_ref,
    dest_ref,
    block_ref,
    gain_ref,
    norm_ref,
    x_ref,
    w_ref,
    out_ref,
    x_v,
    w_v,
    acc,
    trig,
    norm,
    mine,
    held,
    meta_mine,
    meta_held,
    meta_smem,
    x_sem,
    w_sem,
    z_sem,
    pass_sem,
    relay_sem,
    recv_sem,
    meta_send,
    meta_recv,
    meta_local,
):
    n_inst, n_dp = sizes
    units, tokens, width = mine.shape[0], x_v.shape[0], x_v.shape[1]
    features = w_ref.shape[0]
    latent = norm_ref.shape[1]
    half = (features - latent) // 2
    capacity = 2 * tokens // n_dp
    n_y = n_dp // 2
    steps = len(CHUNKS)
    first_row = [sum(CHUNKS[:c]) for c in range(len(CHUNKS))]

    group = lax.axis_index("groups")
    inst = lax.axis_index("inst")
    rank = lax.axis_index("dp")
    far = lax.rem(inst + n_inst // 2, n_inst)
    y = rank // 2
    core = lax.rem(rank, 2)
    sibling = y * 2 + 1 - core
    columns = [lax.rem(y + j, n_y) * 2 + core for j in range(1, n_y)]

    w_copies = [
        pltpu.make_async_copy(
            w_ref.at[:, pl.ds(k * KTILE, KTILE)], w_v.at[:, pl.ds(k * KTILE, KTILE)], w_sem.at[k]
        )
        for k in range(width // KTILE)
    ]
    x_copies = [
        pltpu.make_async_copy(
            x_ref.at[pl.ds(first_row[c], CHUNKS[c]), :],
            x_v.at[pl.ds(first_row[c], CHUNKS[c]), :],
            x_sem.at[c],
        )
        for c in range(len(CHUNKS))
    ]
    x_copies[0].start()
    for copy in w_copies:
        copy.start()
    for copy in x_copies[1:]:
        copy.start()

    barrier = pltpu.get_barrier_semaphore()
    for e in range(n_dp):
        pl.semaphore_signal(barrier, inc=1, device_id=(group, far, e), device_id_type=MESH)
    for other in [sibling] + columns:
        pl.semaphore_signal(barrier, inc=1, device_id=(group, inst, other), device_id_type=MESH)

    starts = []
    total = jnp.int32(0)
    for k in range(n_dp):
        starts.append(total)
        total = total + len_ref[0, 0, k]
    row = lax.broadcasted_iota(jnp.int32, meta_mine.shape, 0)
    lane = lax.broadcasted_iota(jnp.int32, meta_mine.shape, 1)
    table = jnp.zeros(meta_mine.shape, jnp.int32)
    for k in range(n_dp):
        entry = jnp.where(
            lane == 0,
            starts[k],
            jnp.where(lane == 1, len_ref[0, 0, k], block_ref[0, 0, k]),
        )
        table = jnp.where(row == dest_ref[0, 0, k], entry, table)
    meta_mine[...] = table

    which = lax.broadcasted_iota(jnp.int32, (half, tokens), 0).astype(jnp.float32)
    inverse = jnp.exp(which * jnp.float32(-math.log(10000.0) / half))
    at = lax.broadcasted_iota(jnp.int32, (half, tokens), 1)
    begin = jnp.zeros((half, tokens), jnp.int32)
    for k in range(1, n_dp):
        begin = jnp.where(at >= starts[k], starts[k], begin)
    angle = (at - begin).astype(jnp.float32) * inverse
    trig[pl.ds(0, half), :] = jnp.cos(angle)
    trig[pl.ds(half, half), :] = jnp.sin(angle)

    norm[...] = jnp.broadcast_to(norm_ref[...], (LANES, latent)).T

    def compute(c):
        rows = CHUNKS[c]
        span = pl.ds(first_row[c], rows)
        x_copies[c].wait()
        squares = jnp.zeros((rows, LANES), jnp.float32)
        for k in range(width // KTILE):
            if c == 0:
                w_copies[k].wait()
            cols = pl.ds(k * KTILE, KTILE)
            values = x_v[span, cols].astype(jnp.float32)
            powers = values * values
            for j in range(KTILE // LANES):
                squares = squares + powers[:, j * LANES : (j + 1) * LANES]
            scaled = (values * gain_ref[:, cols]).astype(jnp.bfloat16)
            product = lax.dot_general(
                w_v[:, cols],
                scaled,
                (((1,), (1,)), ((), ())),
                preferred_element_type=jnp.float32,
            )
            if k == 0:
                acc[:, pl.ds(0, rows)] = product
            else:
                acc[:, pl.ds(0, rows)] += product
        squares = jnp.sum(squares.T, axis=0, keepdims=True)
        scale = lax.rsqrt(squares * (1.0 / width) + 1e-06)
        compressed = acc[pl.ds(0, latent), pl.ds(0, rows)] * scale
        power = jnp.mean(compressed * compressed, axis=0, keepdims=True)
        compressed = compressed * lax.rsqrt(power + 1e-06)
        a = acc[pl.ds(latent, half), pl.ds(0, rows)] * scale
        b = acc[pl.ds(latent + half, half), pl.ds(0, rows)] * scale
        cosine, sine = trig[pl.ds(0, half), span], trig[pl.ds(half, half), span]
        turned = jnp.concatenate([a * cosine - b * sine, a * sine + b * cosine], axis=0)
        for u in range(rows // LANES):
            lanes = slice(u * LANES, (u + 1) * LANES)
            unit = first_row[c] // LANES + u
            mine[unit, pl.ds(0, latent), :] = (compressed[:, lanes] * norm[...]).astype(jnp.bfloat16)
            mine[unit, pl.ds(latent, 2 * half), :] = turned[:, lanes].astype(jnp.bfloat16)

    def chunk_of(c):
        return pl.ds(first_row[c] // LANES, CHUNKS[c] // LANES)

    def send_far(s):
        return pltpu.make_async_remote_copy(
            src_ref=mine.at[chunk_of(s)],
            dst_ref=held.at[rank, chunk_of(s)],
            send_sem=z_sem.at[s],
            recv_sem=recv_sem.at[rank, s],
            device_id=(group, far, rank),
            device_id_type=MESH,
        )

    def pass_on(c, source, target, sem):
        return pltpu.make_async_remote_copy(
            src_ref=held.at[source, chunk_of(c)],
            dst_ref=held.at[source, chunk_of(c)],
            send_sem=sem,
            recv_sem=recv_sem.at[source, c],
            device_id=(group, inst, target),
            device_id_type=MESH,
        )

    def send_meta(e, source):
        return pltpu.make_async_remote_copy(
            src_ref=meta_mine,
            dst_ref=meta_held.at[source],
            send_sem=meta_send.at[e],
            recv_sem=meta_recv.at[source],
            device_id=(group, far, e),
            device_id_type=MESH,
        )

    for c in range(len(CHUNKS)):
        compute(c)
        if c == 0:
            pl.semaphore_wait(barrier, n_dp + 1 + len(columns))
        send_far(c).start()
        if c == 0:
            for e in range(n_dp):
                send_meta(e, rank).start()

    def spread(c):
        send_far(c).wait_recv()
        for j, other in enumerate(columns):
            pass_on(c, rank, other, pass_sem.at[j, c]).start()
        pass_on(c, rank, sibling, pass_sem.at[n_y - 1, c]).start()

    def relay(c):
        for j, other in enumerate(columns):
            pass_on(c, other, other, relay_sem.at[j, c]).wait_recv()
            pass_on(c, other, sibling, relay_sem.at[j, c]).start()

    for c in range(steps):
        spread(c)
        if c == 0:
            for d in range(n_dp):
                send_meta(0, d).wait_recv()
            to_smem = pltpu.make_async_copy(meta_held, meta_smem, meta_local)
            to_smem.start()
            to_smem.wait()
        if c > 0:
            relay(c - 1)
    relay(steps - 1)
    for c in range(steps):
        for source in [sibling] + [o // 2 * 2 + 1 - core for o in columns]:
            pass_on(c, source, sibling, pass_sem.at[0, c]).wait_recv()

    together = max(1, LANES // capacity)
    for first in range(0, n_dp, together):
        blocks = []
        for b in range(first, first + together):
            page = b * (capacity // BLOCK)
            source, start, count = jnp.int32(0), jnp.int32(0), jnp.int32(0)
            for d in range(n_dp):
                here = meta_smem[d, rank, 2] == page
                source = jnp.where(here, d, source)
                start = jnp.where(here, meta_smem[d, rank, 0], start)
                count = jnp.where(here, meta_smem[d, rank, 1], count)
            in_row = lax.broadcasted_iota(jnp.int32, (tokens, capacity), 0)
            out_row = lax.broadcasted_iota(jnp.int32, (tokens, capacity), 1)
            pick = (in_row == out_row + start) & (out_row < count)
            pick = jnp.where(pick, 1.0, 0.0).astype(jnp.bfloat16)
            rows = jnp.concatenate([held[source, u] for u in range(units)], axis=1)
            blocks.append(jnp.dot(rows, pick, preferred_element_type=jnp.float32))
        block = blocks[0] if together == 1 else jnp.concatenate(blocks, axis=1)
        out_ref[:, pl.ds(first * capacity, together * capacity)] = block.astype(out_ref.dtype)

    for e in range(n_dp):
        send_meta(e, rank).wait_send()
    for c in range(steps):
        send_far(c).wait_send()
        for j, other in enumerate(columns):
            pass_on(c, rank, other, pass_sem.at[j, c]).wait_send()
            pass_on(c, other, sibling, relay_sem.at[j, c]).wait_send()
        pass_on(c, rank, sibling, pass_sem.at[n_y - 1, c]).wait_send()


def on_device(
    n_inst, n_dp, hidden, input_gain, w_latent, latent_norm_gain, req_len, req_dest, req_block
):
    tokens, width = hidden.shape
    lat = w_latent.shape[1]
    latent = latent_norm_gain.shape[0]
    units = tokens // LANES
    steps = len(CHUNKS)
    n_y = n_dp // 2
    meta_rows = max(8, n_dp)
    smem = pl.BlockSpec(memory_space=pltpu.SMEM)
    vmem = pl.BlockSpec(memory_space=pltpu.VMEM)
    hbm = pl.BlockSpec(memory_space=pl.ANY)
    dma = pltpu.SemaphoreType.DMA
    placed = pl.pallas_call(
        functools.partial(kernel, (n_inst, n_dp)),
        out_shape=jax.ShapeDtypeStruct((lat, 2 * tokens), jnp.bfloat16),
        in_specs=[smem, smem, smem, vmem, vmem, hbm, hbm],
        out_specs=vmem,
        scratch_shapes=[
            pltpu.VMEM((tokens, width), jnp.bfloat16),
            pltpu.VMEM((lat, width), jnp.bfloat16),
            pltpu.VMEM((lat, max(CHUNKS)), jnp.float32),
            pltpu.VMEM((lat - latent, tokens), jnp.float32),
            pltpu.VMEM((latent, LANES), jnp.float32),
            pltpu.VMEM((units, lat, LANES), jnp.bfloat16),
            pltpu.VMEM((n_dp, units, lat, LANES), jnp.bfloat16),
            pltpu.VMEM((meta_rows, LANES), jnp.int32),
            pltpu.VMEM((n_dp, meta_rows, LANES), jnp.int32),
            pltpu.SMEM((n_dp, meta_rows, LANES), jnp.int32),
            dma((len(CHUNKS),)),
            dma((width // KTILE,)),
            dma((steps,)),
            dma((n_y, steps)),
            dma((n_y, steps)),
            dma((n_dp, steps)),
            dma((n_dp,)),
            dma((n_dp,)),
            dma,
        ],
        compiler_params=pltpu.CompilerParams(
            collective_id=0, has_side_effects=True, vmem_limit_bytes=48 * 1024 * 1024
        ),
        cost_estimate=pl.CostEstimate(
            flops=2 * tokens * width * lat,
            bytes_accessed=2 * (tokens * width + width * lat + 2 * tokens * lat),
            transcendentals=tokens * LANES,
        ),
    )(
        req_len,
        req_dest,
        req_block,
        input_gain.reshape(1, width),
        latent_norm_gain.reshape(1, latent),
        hidden,
        w_latent.T,
    )
    return placed.T


def solution(mesh):
    placed = (
        P(("groups", "inst", "dp"), None),
        P(),
        P(),
        P(),
        P(("groups", "inst"), "dp", None),
        P(("groups", "inst"), "dp", None),
        P(("groups", "inst"), "dp", None),
    )
    return jax.shard_map(
        functools.partial(on_device, mesh.shape["inst"], mesh.shape["dp"]),
        mesh=mesh,
        in_specs=placed,
        out_specs=P(("groups", "inst", "dp"), None),
        check_vma=False,
    )
```

```python
import functools
import math

import jax
import jax.numpy as jnp
from jax import lax
from jax.experimental import pallas as pl
from jax.experimental.pallas import tpu as pltpu
from jax.sharding import PartitionSpec as P

BLOCK = 64
LANES = 128
MESH = pl.DeviceIdType.MESH
CHUNKS = (128, 128, 128, 128)
KTILE = 1792


def kernel(
    sizes,
    len_ref,
    dest_ref,
    block_ref,
    gain_ref,
    norm_ref,
    x_ref,
    w_ref,
    out_ref,
    x_v,
    w_v,
    acc,
    trig,
    norm,
    mine,
    held,
    meta_mine,
    meta_held,
    meta_smem,
    x_sem,
    w_sem,
    z_sem,
    pass_sem,
    relay_sem,
    recv_sem,
    meta_send,
    meta_recv,
    meta_local,
):
    n_inst, n_dp = sizes
    units, tokens, width = mine.shape[0], x_v.shape[0], x_v.shape[1]
    features = w_ref.shape[0]
    latent = norm_ref.shape[1]
    half = (features - latent) // 2
    capacity = 2 * tokens // n_dp
    n_y = n_dp // 2
    steps = len(CHUNKS)
    first_row = [sum(CHUNKS[:c]) for c in range(len(CHUNKS))]

    group = lax.axis_index("groups")
    inst = lax.axis_index("inst")
    rank = lax.axis_index("dp")
    far = lax.rem(inst + n_inst // 2, n_inst)
    y = rank // 2
    core = lax.rem(rank, 2)
    sibling = y * 2 + 1 - core
    columns = [lax.rem(y + j, n_y) * 2 + core for j in range(1, n_y)]

    w_copies = [
        pltpu.make_async_copy(
            w_ref.at[:, pl.ds(k * KTILE, KTILE)], w_v.at[:, pl.ds(k * KTILE, KTILE)], w_sem.at[k]
        )
        for k in range(width // KTILE)
    ]
    x_copies = [
        pltpu.make_async_copy(
            x_ref.at[pl.ds(first_row[c], CHUNKS[c]), :],
            x_v.at[pl.ds(first_row[c], CHUNKS[c]), :],
            x_sem.at[c],
        )
        for c in range(len(CHUNKS))
    ]
    x_copies[0].start()
    for copy in w_copies:
        copy.start()
    for copy in x_copies[1:]:
        copy.start()

    barrier = pltpu.get_barrier_semaphore()
    for e in range(n_dp):
        pl.semaphore_signal(barrier, inc=1, device_id=(group, far, e), device_id_type=MESH)
    for other in [sibling] + columns:
        pl.semaphore_signal(barrier, inc=1, device_id=(group, inst, other), device_id_type=MESH)

    starts = []
    total = jnp.int32(0)
    for k in range(n_dp):
        starts.append(total)
        total = total + len_ref[0, 0, k]
    row = lax.broadcasted_iota(jnp.int32, meta_mine.shape, 0)
    lane = lax.broadcasted_iota(jnp.int32, meta_mine.shape, 1)
    table = jnp.zeros(meta_mine.shape, jnp.int32)
    for k in range(n_dp):
        entry = jnp.where(
            lane == 0,
            starts[k],
            jnp.where(lane == 1, len_ref[0, 0, k], block_ref[0, 0, k]),
        )
        table = jnp.where(row == dest_ref[0, 0, k], entry, table)
    meta_mine[...] = table

    which = lax.broadcasted_iota(jnp.int32, (half, tokens), 0).astype(jnp.float32)
    inverse = jnp.exp(which * jnp.float32(-math.log(10000.0) / half))
    at = lax.broadcasted_iota(jnp.int32, (half, tokens), 1)
    begin = jnp.zeros((half, tokens), jnp.int32)
    for k in range(1, n_dp):
        begin = jnp.where(at >= starts[k], starts[k], begin)
    angle = (at - begin).astype(jnp.float32) * inverse
    trig[pl.ds(0, half), :] = jnp.cos(angle)
    trig[pl.ds(half, half), :] = jnp.sin(angle)

    norm[...] = jnp.broadcast_to(norm_ref[...], (LANES, latent)).T

    def compute(c):
        rows = CHUNKS[c]
        span = pl.ds(first_row[c], rows)
        x_copies[c].wait()
        squares = jnp.zeros((rows, LANES), jnp.float32)
        for k in range(width // KTILE):
            if c == 0:
                w_copies[k].wait()
            cols = pl.ds(k * KTILE, KTILE)
            values = x_v[span, cols].astype(jnp.float32)
            powers = values * values
            for j in range(KTILE // LANES):
                squares = squares + powers[:, j * LANES : (j + 1) * LANES]
            scaled = (values * gain_ref[:, cols]).astype(jnp.bfloat16)
            product = lax.dot_general(
                w_v[:, cols],
                scaled,
                (((1,), (1,)), ((), ())),
                preferred_element_type=jnp.float32,
            )
            if k == 0:
                acc[:, pl.ds(0, rows)] = product
            else:
                acc[:, pl.ds(0, rows)] += product
        squares = jnp.sum(squares.T, axis=0, keepdims=True)
        scale = lax.rsqrt(squares * (1.0 / width) + 1e-06)
        compressed = acc[pl.ds(0, latent), pl.ds(0, rows)] * scale
        power = jnp.mean(compressed * compressed, axis=0, keepdims=True)
        compressed = compressed * lax.rsqrt(power + 1e-06)
        a = acc[pl.ds(latent, half), pl.ds(0, rows)] * scale
        b = acc[pl.ds(latent + half, half), pl.ds(0, rows)] * scale
        cosine, sine = trig[pl.ds(0, half), span], trig[pl.ds(half, half), span]
        turned = jnp.concatenate([a * cosine - b * sine, a * sine + b * cosine], axis=0)
        for u in range(rows // LANES):
            lanes = slice(u * LANES, (u + 1) * LANES)
            unit = first_row[c] // LANES + u
            mine[unit, pl.ds(0, latent), :] = (compressed[:, lanes] * norm[...]).astype(jnp.bfloat16)
            mine[unit, pl.ds(latent, 2 * half), :] = turned[:, lanes].astype(jnp.bfloat16)

    def chunk_of(c):
        return pl.ds(first_row[c] // LANES, CHUNKS[c] // LANES)

    def send_far(s):
        return pltpu.make_async_remote_copy(
            src_ref=mine.at[chunk_of(s)],
            dst_ref=held.at[rank, chunk_of(s)],
            send_sem=z_sem.at[s],
            recv_sem=recv_sem.at[rank, s],
            device_id=(group, far, rank),
            device_id_type=MESH,
        )

    def pass_on(c, source, target, sem):
        return pltpu.make_async_remote_copy(
            src_ref=held.at[source, chunk_of(c)],
            dst_ref=held.at[source, chunk_of(c)],
            send_sem=sem,
            recv_sem=recv_sem.at[source, c],
            device_id=(group, inst, target),
            device_id_type=MESH,
        )

    def send_meta(e, source):
        return pltpu.make_async_remote_copy(
            src_ref=meta_mine,
            dst_ref=meta_held.at[source],
            send_sem=meta_send.at[e],
            recv_sem=meta_recv.at[source],
            device_id=(group, far, e),
            device_id_type=MESH,
        )

    for c in range(len(CHUNKS)):
        compute(c)
        if c == 0:
            pl.semaphore_wait(barrier, n_dp + 1 + len(columns))
        send_far(c).start()
        if c == 0:
            for e in range(n_dp):
                send_meta(e, rank).start()

    def spread(c):
        send_far(c).wait_recv()
        for j, other in enumerate(columns):
            pass_on(c, rank, other, pass_sem.at[j, c]).start()
        pass_on(c, rank, sibling, pass_sem.at[n_y - 1, c]).start()

    def relay(c):
        for j, other in enumerate(columns):
            pass_on(c, other, other, relay_sem.at[j, c]).wait_recv()
            pass_on(c, other, sibling, relay_sem.at[j, c]).start()

    for c in range(steps):
        spread(c)
        if c == 0:
            for d in range(n_dp):
                send_meta(0, d).wait_recv()
            to_smem = pltpu.make_async_copy(meta_held, meta_smem, meta_local)
            to_smem.start()
            to_smem.wait()
        if c > 0:
            relay(c - 1)
    relay(steps - 1)
    for c in range(steps):
        for source in [sibling] + [o // 2 * 2 + 1 - core for o in columns]:
            pass_on(c, source, sibling, pass_sem.at[0, c]).wait_recv()

    together = max(1, LANES // capacity)
    for first in range(0, n_dp, together):
        blocks = []
        for b in range(first, first + together):
            page = b * (capacity // BLOCK)
            source, start, count = jnp.int32(0), jnp.int32(0), jnp.int32(0)
            for d in range(n_dp):
                here = meta_smem[d, rank, 2] == page
                source = jnp.where(here, d, source)
                start = jnp.where(here, meta_smem[d, rank, 0], start)
                count = jnp.where(here, meta_smem[d, rank, 1], count)
            in_row = lax.broadcasted_iota(jnp.int32, (tokens, capacity), 0)
            out_row = lax.broadcasted_iota(jnp.int32, (tokens, capacity), 1)
            pick = (in_row == out_row + start) & (out_row < count)
            pick = jnp.where(pick, 1.0, 0.0).astype(jnp.bfloat16)
            rows = jnp.concatenate([held[source, u] for u in range(units)], axis=1)
            blocks.append(jnp.dot(rows, pick, preferred_element_type=jnp.float32))
        block = blocks[0] if together == 1 else jnp.concatenate(blocks, axis=1)
        out_ref[:, pl.ds(first * capacity, together * capacity)] = block.astype(out_ref.dtype)

    for e in range(n_dp):
        send_meta(e, rank).wait_send()
    for c in range(steps):
        send_far(c).wait_send()
        for j, other in enumerate(columns):
            pass_on(c, rank, other, pass_sem.at[j, c]).wait_send()
            pass_on(c, other, sibling, relay_sem.at[j, c]).wait_send()
        pass_on(c, rank, sibling, pass_sem.at[n_y - 1, c]).wait_send()


def on_device(
    n_inst, n_dp, hidden, input_gain, w_latent, latent_norm_gain, req_len, req_dest, req_block
):
    tokens, width = hidden.shape
    lat = w_latent.shape[1]
    latent = latent_norm_gain.shape[0]
    units = tokens // LANES
    steps = len(CHUNKS)
    n_y = n_dp // 2
    meta_rows = max(8, n_dp)
    smem = pl.BlockSpec(memory_space=pltpu.SMEM)
    vmem = pl.BlockSpec(memory_space=pltpu.VMEM)
    hbm = pl.BlockSpec(memory_space=pl.ANY)
    dma = pltpu.SemaphoreType.DMA
    placed = pl.pallas_call(
        functools.partial(kernel, (n_inst, n_dp)),
        out_shape=jax.ShapeDtypeStruct((lat, 2 * tokens), jnp.bfloat16),
        in_specs=[smem, smem, smem, vmem, vmem, hbm, hbm],
        out_specs=vmem,
        scratch_shapes=[
            pltpu.VMEM((tokens, width), jnp.bfloat16),
            pltpu.VMEM((lat, width), jnp.bfloat16),
            pltpu.VMEM((lat, max(CHUNKS)), jnp.float32),
            pltpu.VMEM((lat - latent, tokens), jnp.float32),
            pltpu.VMEM((latent, LANES), jnp.float32),
            pltpu.VMEM((units, lat, LANES), jnp.bfloat16),
            pltpu.VMEM((n_dp, units, lat, LANES), jnp.bfloat16),
            pltpu.VMEM((meta_rows, LANES), jnp.int32),
            pltpu.VMEM((n_dp, meta_rows, LANES), jnp.int32),
            pltpu.SMEM((n_dp, meta_rows, LANES), jnp.int32),
            dma((len(CHUNKS),)),
            dma((width // KTILE,)),
            dma((steps,)),
            dma((n_y, steps)),
            dma((n_y, steps)),
            dma((n_dp, steps)),
            dma((n_dp,)),
            dma((n_dp,)),
            dma,
        ],
        compiler_params=pltpu.CompilerParams(
            collective_id=0, has_side_effects=True, vmem_limit_bytes=48 * 1024 * 1024
        ),
        cost_estimate=pl.CostEstimate(
            flops=2 * tokens * width * lat,
            bytes_accessed=2 * (tokens * width + width * lat + 2 * tokens * lat),
            transcendentals=tokens * LANES,
        ),
    )(
        req_len,
        req_dest,
        req_block,
        input_gain.reshape(1, width),
        latent_norm_gain.reshape(1, latent),
        hidden,
        w_latent.T,
    )
    return placed.T


def solution(mesh):
    placed = (
        P(("groups", "inst", "dp"), None),
        P(),
        P(),
        P(),
        P(("groups", "inst"), "dp", None),
        P(("groups", "inst"), "dp", None),
        P(("groups", "inst"), "dp", None),
    )
    return jax.shard_map(
        functools.partial(on_device, mesh.shape["inst"], mesh.shape["dp"]),
        mesh=mesh,
        in_specs=placed,
        out_specs=P(("groups", "inst", "dp"), None),
        check_vma=False,
    )
```
